32 devices in a mesh: section: 2 (over core), req: 16 (over z, y, x).
Axes of the slice: x: 2, y: 2, z: 4, core: 2. Of those that a mesh axis runs over, the one named last changes fastest.
Arguments:
- section_in: bfloat16 [2, 16, 32, 1152], P('section', 'req'), may hold values from -24 to 24
- patch_index: int32 [2, 16], P('section', 'req'), may hold values from 0 to 3
- stale_kv: bfloat16 [2, 16, 128, 2304], P('section', 'req'), may hold values from -400 to 400
- modulation: float32 [2, 16, 6, 1152], P('section', 'req'), may hold values from -4 to 4
- final_mod: float32 [16, 2, 1152], P('req'), may hold values from -4 to 4
- qkv_blocks: bfloat16 [2, 16, 1152, 864], P('section', 'req'), may hold values from -1 to 1, as said below
- out_blocks: bfloat16 [2, 16, 1152, 288], P('section', 'req'), may hold values from -1 to 1, as said below
- up_blocks: bfloat16 [2, 16, 1152, 1152], P('section', 'req'), may hold values from -1 to 1, as said below
- down_blocks: bfloat16 [2, 16, 1152, 1152], P('section', 'req'), may hold values from -1 to 1, as said below
- final_weight: bfloat16 [1152, 16], replicated, may hold values from -0.1875 to 0.1875
- noisy_latent: float32 [16, 512], P('req', 'section'), may hold values from -6 to 6
- time_index: int32 [16], P('req'), may hold values from 100 to 499
- time_gap: int32 [16], P('req'), may hold values from 10 to 40
Outputs:
- fresh_kv: bfloat16 [2, 16, 32, 2304], P('section', 'req')
- next_input: bfloat16 [16, 32, 1152], P('req', 'section')
- noise_pred: float32 [16, 512], P('req', 'section')
- denoised: float32 [16, 512], P('req', 'section')
The draws below stay inside these ranges and needn't reach their ends.
Inputs may be any that keep to these rules, and one draw needn't show every extreme that they name: qkv_blocks[s, r] equals qkv_blocks[s, r mod 4]. out_blocks[s, r] equals out_blocks[s, r mod 4]. up_blocks[s, r] equals up_blocks[s, r mod 4]. down_blocks[s, r] equals down_blocks[s, r mod 4].
All inputs are finite; a program needn't handle non-finite values.
Results may differ from the reference program's by a relative error of at most 0.0093.
Values may be sent and summed in bfloat16 or wider, within the bound.
No kernel may reach another device: no remote copies, remote signals or barrier semaphores. Data moves between devices by JAX's collectives and lax.ppermute only.
A program may use at most 64 MiB of HBM per device.

```python
import math
import jax
import jax.numpy as jnp
from jax import lax

D = 1152
HEADS = 16
FF = 4608
CH = 16
PATCHES = 4
UNIT_GROUPS = 4
PATCH_TOK = 32
LAT_TOK = 128
LAYERS = 2
REQS = 16
WEIGHT_COPIES = 16


def clipped_normal(key, extent):
    return jnp.clip(jax.random.normal(key, extent, jnp.float32), -4.0, 4.0)


def tiled_blocks(key, rows_in, columns, fan_in):
    blocks = clipped_normal(key, (LAYERS, UNIT_GROUPS, rows_in, columns)) * fan_in ** (-0.5)
    copies = jnp.arange(WEIGHT_COPIES, dtype=jnp.int32) % UNIT_GROUPS
    return jnp.take(blocks, copies, axis=1).astype(jnp.bfloat16)


def draw_section_in(key, part):
    seeded = jax.random.fold_in(key, 11)
    key_row, key_col, key_main = jax.random.split(seeded, 3)
    extent = (LAYERS, REQS, PATCH_TOK, D)
    row_scale = jnp.exp(jax.random.uniform(key_row, (LAYERS, REQS, PATCH_TOK, 1), jnp.float32, math.log(0.3), math.log(3.0)))
    column_scale = jnp.exp(jax.random.uniform(key_col, (1, 1, 1, D), jnp.float32, math.log(0.5), math.log(2.0)))
    entries = clipped_normal(key_main, extent)
    return (entries * row_scale * column_scale).astype(jnp.bfloat16)


def draw_stale_kv(key, part):
    seeded = jax.random.fold_in(key, 37)
    key_keys, key_values = jax.random.split(seeded, 2)
    key_rows = 2.0 * clipped_normal(key_keys, (LAYERS, REQS, LAT_TOK, D))
    value_rows = 1.5 * clipped_normal(key_values, (LAYERS, REQS, LAT_TOK, D))
    return jnp.concatenate([key_rows, value_rows], axis=-1).astype(jnp.bfloat16)


def draw_qkv_blocks(key, part):
    return tiled_blocks(jax.random.fold_in(key, 41), D, 3 * D // UNIT_GROUPS, D)


def draw_out_blocks(key, part):
    return tiled_blocks(jax.random.fold_in(key, 43), D, D // UNIT_GROUPS, D)


def draw_up_blocks(key, part):
    return tiled_blocks(jax.random.fold_in(key, 47), D, FF // UNIT_GROUPS, D)


def draw_down_blocks(key, part):
    return tiled_blocks(jax.random.fold_in(key, 53), FF // UNIT_GROUPS, D, FF)


def touch_ends(values, rng, low, largest):
    longest = values.shape.index(max(values.shape))
    spots = []
    for shift in (0, 1):
        where = [jax.random.randint(jax.random.fold_in(rng, axis), (), 0, length) for axis, length in enumerate(values.shape)]
        where[longest] = (where[longest] + shift) % values.shape[longest]
        spots.append(tuple(where))
    return values.at[spots[0]].set(low).at[spots[1]].set(largest)


def block_scale(own_key, dims, shards, low, high):
    def one(position, blocks):
        steps = jax.random.uniform(jax.random.fold_in(jax.random.fold_in(own_key, 6), position), (blocks,), jnp.float32, low / len(shards), high / len(shards))
        return jnp.repeat(jnp.exp(steps), dims[position] // blocks).reshape((-1,) + (1,) * (len(dims) - position - 1))

    level = one(*shards[0])
    for cut in shards[1:]:
        level = level * one(*cut)
    return level


def normal_values(own_key, dims, scale, limit, shards=(), held_as=jnp.bfloat16):
    values = jax.random.normal(own_key, dims, jnp.float32) * scale
    if len(shards) > 0:
        values = block_scale(own_key, dims, shards, -0.22, 0.18) * values
    return jnp.clip(values, min=-limit, max=limit).astype(held_as)


def setup_inputs(seed: int = 0) -> dict:
    arg_keys = jax.random.split(jax.random.key(seed), 14)
    return {
        "section_in": draw_section_in(jax.random.fold_in(arg_keys[13], 71), 0),
        "patch_index": touch_ends(jax.random.randint(arg_keys[1], (LAYERS, REQS), 0, PATCHES), jax.random.fold_in(arg_keys[1], 1), 0, PATCHES - 1).astype(jnp.int32),
        "stale_kv": draw_stale_kv(jax.random.fold_in(arg_keys[13], 71), 0),
        "modulation": normal_values(arg_keys[3], (LAYERS, REQS, 6, D), 1.0, 4.0, ((0, 2), (1, 16)), jnp.float32),
        "final_mod": normal_values(arg_keys[4], (REQS, 2, D), 1.0, 4.0, ((0, 16),), jnp.float32),
        "qkv_blocks": draw_qkv_blocks(jax.random.fold_in(arg_keys[13], 71), 0),
        "out_blocks": draw_out_blocks(jax.random.fold_in(arg_keys[13], 71), 0),
        "up_blocks": draw_up_blocks(jax.random.fold_in(arg_keys[13], 71), 0),
        "down_blocks": draw_down_blocks(jax.random.fold_in(arg_keys[13], 71), 0),
        "final_weight": normal_values(arg_keys[9], (D, CH), D ** -0.5, 0.1875),
        "noisy_latent": normal_values(arg_keys[10], (REQS, PATCH_TOK * CH), 1.0, 6.0, ((0, 16), (1, 2)), jnp.float32),
        "time_index": touch_ends(jax.random.randint(arg_keys[11], (REQS,), 100, 500), jax.random.fold_in(arg_keys[11], 1), 100, 499).astype(jnp.int32),
        "time_gap": touch_ends(jax.random.randint(arg_keys[12], (REQS,), 10, 41), jax.random.fold_in(arg_keys[12], 1), 10, 40).astype(jnp.int32),
    }


NORM_EPS = 1e-06
BETA_LOW = 0.0001
BETA_HIGH = 0.02

def layer_norm(values):
    average = lax.optimization_barrier(jnp.mean(values, axis=-1, keepdims=True))
    centred = values - average
    spread = lax.optimization_barrier(jnp.mean(centred * centred, axis=-1, keepdims=True))
    return centred * lax.rsqrt(spread + NORM_EPS)

def alpha_bar(step_index):
    moment = step_index.astype(jnp.float32)
    return jnp.exp(-(BETA_LOW * (moment + 1.0) + (BETA_HIGH - BETA_LOW) * moment * (moment + 1.0) / 1998.0))

def attend(queries, fresh_keys, fresh_values, stale_rows, patch_at):
    fresh_count = queries.shape[0]
    model_width = queries.shape[1]
    head_size = model_width // HEADS
    fresh_rows = jnp.concatenate([fresh_keys, fresh_values], axis=1)
    start = (patch_at * fresh_count).astype(jnp.int32)
    all_rows = lax.dynamic_update_slice(stale_rows, fresh_rows, (start, jnp.zeros((), jnp.int32)))
    key_rows = all_rows[:, :model_width].astype(jnp.float32)
    value_rows = all_rows[:, model_width:].astype(jnp.float32)
    scores = jnp.einsum('qhd,khd->hqk', queries.astype(jnp.float32).reshape(fresh_count, HEADS, head_size), key_rows.reshape(-1, HEADS, head_size)) * head_size ** (-0.5)
    highest = lax.optimization_barrier(jnp.max(scores, axis=-1, keepdims=True))
    raised = jnp.exp(scores - highest)
    attention_weights = (raised / lax.optimization_barrier(jnp.sum(raised, axis=-1, keepdims=True))).astype(jnp.bfloat16)
    mixed = jnp.einsum('hqk,khd->qhd', attention_weights.astype(jnp.float32), value_rows.reshape(-1, HEADS, head_size))
    return mixed.reshape(fresh_count, model_width).astype(jnp.bfloat16)

def layer_step(hidden, stale_rows, mods, patch_at, w_qkv, w_out, w_up, w_down):
    fresh_count = hidden.shape[0]
    model_width = hidden.shape[1]
    residual = hidden.astype(jnp.float32)
    normed = (layer_norm(residual) * (1.0 + mods[1]) + mods[0]).astype(jnp.bfloat16)
    joined = jnp.dot(normed, w_qkv, preferred_element_type=jnp.float32).astype(jnp.bfloat16)
    joined = joined.reshape(fresh_count, UNIT_GROUPS, 3, model_width // UNIT_GROUPS)
    queries = joined[:, :, 0].reshape(fresh_count, model_width)
    fresh_keys = joined[:, :, 1].reshape(fresh_count, model_width)
    fresh_values = joined[:, :, 2].reshape(fresh_count, model_width)
    mixed = attend(queries, fresh_keys, fresh_values, stale_rows, patch_at)
    projected = jnp.dot(mixed, w_out, preferred_element_type=jnp.float32).astype(jnp.bfloat16)
    projected = lax.optimization_barrier(projected)
    after_attention = residual + mods[2] * projected.astype(jnp.float32)
    middle = (layer_norm(after_attention) * (1.0 + mods[4]) + mods[3]).astype(jnp.bfloat16)
    total = jnp.zeros(after_attention.shape, jnp.float32)
    for group in range(UNIT_GROUPS):
        inner = jax.nn.gelu(jnp.dot(middle, w_up[group], preferred_element_type=jnp.float32), approximate=True).astype(jnp.bfloat16)
        partial_out = jnp.dot(inner, w_down[group], preferred_element_type=jnp.float32).astype(jnp.bfloat16)
        partial_out = lax.optimization_barrier(partial_out)
        total = total + partial_out.astype(jnp.float32)
    layer_out = (after_attention + mods[5] * total).astype(jnp.bfloat16)
    return (layer_out, jnp.concatenate([fresh_keys, fresh_values], axis=1))

def reference(section_in, patch_index, stale_kv, modulation, final_mod, qkv_blocks, out_blocks, up_blocks, down_blocks, final_weight, noisy_latent, time_index, time_gap):
    layer_outputs = []
    fresh_all = []
    for layer in range(LAYERS):
        w_qkv = jnp.concatenate([qkv_blocks[layer, group] for group in range(UNIT_GROUPS)], axis=1)
        w_out = jnp.concatenate([out_blocks[layer, group] for group in range(UNIT_GROUPS)], axis=1)
        w_up = up_blocks[layer, :UNIT_GROUPS]
        w_down = down_blocks[layer, :UNIT_GROUPS]

        def one_request(items):
            return layer_step(items[0], items[1], items[2], items[3], w_qkv, w_out, w_up, w_down)
        layer_out, fresh = lax.map(one_request, (section_in[layer], stale_kv[layer], modulation[layer], patch_index[layer]))
        layer_outputs.append(layer_out)
        fresh_all.append(fresh)
    final_rows = layer_outputs[1].astype(jnp.float32)
    shifted = (layer_norm(final_rows) * (1.0 + final_mod[:, 1][:, None, :]) + final_mod[:, 0][:, None, :]).astype(jnp.bfloat16)
    noise_pred = jnp.dot(shifted.reshape(-1, D), final_weight, preferred_element_type=jnp.float32).reshape(REQS, PATCH_TOK * CH)
    now_bar = alpha_bar(time_index)[:, None]
    prev_bar = alpha_bar(time_index - time_gap)[:, None]
    clean_latent = (noisy_latent - jnp.sqrt(1.0 - now_bar) * noise_pred) / jnp.sqrt(now_bar)
    denoised = jnp.sqrt(prev_bar) * clean_latent + jnp.sqrt(1.0 - prev_bar) * noise_pred
    return (jnp.stack(fresh_all), layer_outputs[0], noise_pred, denoised)
```

```python
from functools import partial

import jax
import jax.numpy as jnp
from jax import lax
from jax.experimental import pallas as pl
from jax.experimental.pallas import tpu as pltpu
from jax.sharding import PartitionSpec as P

HEADS = 16
UNIT_GROUPS = 4
LANE_ROWS = 16


NORM_EPS = 1e-06
BETA_LOW = 0.0001
BETA_HIGH = 0.02

BF16 = jnp.bfloat16
F32 = jnp.float32
VMEM = pl.BlockSpec(memory_space=pltpu.VMEM)
SMEM = pl.BlockSpec(memory_space=pltpu.SMEM)
PARAMS = pltpu.CompilerParams(vmem_limit_bytes=32 * 1024 * 1024)


def layer_norm(values):
    average = jnp.mean(values, axis=-1, keepdims=True)
    centred = values - average
    spread = jnp.mean(centred * centred, axis=-1, keepdims=True)
    return centred * lax.rsqrt(spread + NORM_EPS)


def alpha_bar(moment):
    return jnp.exp(
        -(BETA_LOW * (moment + 1.0) + (BETA_HIGH - BETA_LOW) * moment * (moment + 1.0) / 1998.0)
    )


def own_block():
    return lax.rem(lax.axis_index("req"), UNIT_GROUPS)


def other_block(block, k):
    return lax.bitwise_xor(block, jnp.int32(k))


def swap(x, k):
    return lax.ppermute(x, "req", [(i, i ^ k) for i in range(lax.axis_size("req"))])


def call(body, outs, *args, smem=0, scratch=()):
    return pl.pallas_call(
        body,
        out_shape=outs,
        in_specs=[SMEM] * smem + [VMEM] * (len(args) - smem),
        out_specs=jax.tree.map(lambda _: VMEM, outs),
        scratch_shapes=list(scratch),
        compiler_params=PARAMS,
    )(*args)


def norm_kernel(hidden, mods, normed):
    values = layer_norm(hidden[...].astype(F32))
    normed[...] = (values * (1.0 + mods[1:2, :]) + mods[0:1, :]).astype(BF16)


def pack_kernel(patch, hidden, mods, stale, *rest):
    outs, packed = rest[:UNIT_GROUPS], rest[UNIT_GROUPS]
    fresh, width = hidden.shape
    part = width // UNIT_GROUPS
    kept = (stale.shape[0] // fresh - 1) * fresh
    patches = stale.shape[0] // fresh
    start = patch[0, 0]
    high = mods[2:6, :].astype(BF16).astype(F32)
    low = mods[2:6, :] - high
    pad = jnp.zeros((4, part), F32)
    for i in range(1, patches):
        source = pl.multiple_of(lax.rem(start + i, patches) * fresh, fresh)
        rows = stale[pl.ds(source, fresh), :]
        for block in range(UNIT_GROUPS):
            at = block * part
            packed[block, (i - 1) * fresh : i * fresh, :] = rows[:, at : at + part]
            packed[block, kept + (i - 1) * fresh : kept + i * fresh, :] = rows[:, width + at : width + at + part]
    for block in range(UNIT_GROUPS):
        at = block * part
        packed[block, 2 * kept : 2 * kept + fresh, :] = hidden[:, at : at + part]
        for other in range(UNIT_GROUPS):
            there = other * part
            rows = jnp.concatenate([high[:, there : there + part], pad, low[:, there : there + part], pad], axis=0)
            base = 2 * kept + fresh + other * LANE_ROWS
            packed[block, base : base + LANE_ROWS, :] = rows.astype(BF16)
    here = own_block()
    for k in range(UNIT_GROUPS):
        outs[k][...] = packed[other_block(here, k)]


def attend_kernel(n0, n1, n2, n3, p0, p1, p2, p3, weight, a0, a1, a2, a3):
    fresh, width = n0.shape
    part = width // UNIT_GROUPS
    heads = HEADS // UNIT_GROUPS
    head_size = part // heads
    kept = (p0.shape[0] - fresh - UNIT_GROUPS * LANE_ROWS) // 2
    tokens = jnp.concatenate([n0[...], n1[...], n2[...], n3[...]], axis=0)
    joined = jnp.dot(tokens, weight[...], preferred_element_type=F32).astype(BF16)
    lane = lax.broadcasted_iota(jnp.int32, (fresh, part), 1)
    inside = [(lane >= h * head_size) & (lane < (h + 1) * head_size) for h in range(heads)]
    mixed = []
    fresh_rows = []
    for m, packed in enumerate((p0, p1, p2, p3)):
        rows = joined[m * fresh : (m + 1) * fresh]
        q, k, v = rows[:, :part], rows[:, part : 2 * part], rows[:, 2 * part :]
        keys = jnp.concatenate([packed[:kept, :], k], axis=0)
        values = jnp.concatenate([packed[kept : 2 * kept, :], v], axis=0)
        zero = jnp.zeros_like(q)
        spread = jnp.concatenate([jnp.where(inside[h], q, zero) for h in range(heads)], axis=0)
        scores = lax.dot_general(
            spread, keys, (((1,), (1,)), ((), ())), preferred_element_type=F32
        ) * head_size ** (-0.5)
        raised = jnp.exp(scores - jnp.max(scores, axis=-1, keepdims=True))
        probs = (raised / jnp.sum(raised, axis=-1, keepdims=True)).astype(BF16)
        out = jnp.dot(probs, values, preferred_element_type=F32)
        total = jnp.where(inside[0], out[:fresh], 0.0)
        for h in range(1, heads):
            total = jnp.where(inside[h], out[h * fresh : (h + 1) * fresh], total)
        mixed.append(total.astype(BF16))
        fresh_rows.append((k, v))
    for k, out in enumerate((a0, a1, a2, a3)):
        for m in range(UNIT_GROUPS):
            out[m * fresh : (m + 1) * fresh, :] = mixed[k ^ m]
        base = UNIT_GROUPS * fresh
        out[base : base + fresh, :] = fresh_rows[k][0]
        out[base + fresh : base + 2 * fresh, :] = fresh_rows[k][1]


def mod_rows(packed, block, row):
    fresh_base = packed.shape[0] - UNIT_GROUPS * LANE_ROWS
    base = pl.multiple_of(fresh_base + block * LANE_ROWS, LANE_ROWS)
    rows = packed[pl.ds(base, LANE_ROWS), :].astype(F32)
    return rows[row - 2 : row - 1] + rows[row + 6 : row + 7]


def project_kernel(a0, a1, a2, a3, p0, p1, p2, p3, weight, h1, sent, fresh_kv):
    part = weight.shape[1]
    width = weight.shape[0]
    fresh = (a0.shape[0]) // (UNIT_GROUPS + 2)
    count = UNIT_GROUPS * fresh
    residual_at = p0.shape[0] - UNIT_GROUPS * LANE_ROWS - fresh
    here = own_block()
    total = jnp.zeros((count, part), F32)
    for k, mixed in enumerate((a0, a1, a2, a3)):
        rows = pl.ds(pl.multiple_of(other_block(here, k) * part, 32), part)
        total += jnp.dot(mixed[:count, :], weight[rows, :], preferred_element_type=F32)
    projected = total.astype(BF16).astype(F32)
    for m, packed in enumerate((p0, p1, p2, p3)):
        residual = packed[residual_at : residual_at + fresh, :].astype(F32)
        gate = mod_rows(packed, here, 2)
        rows = slice(m * fresh, (m + 1) * fresh)
        value = residual + gate * projected[rows]
        h1[rows, :] = value
        sent[rows, :] = value.astype(BF16)
    for block in range(UNIT_GROUPS):
        for k, mixed in enumerate((a0, a1, a2, a3)):

            @pl.when(other_block(here, k) == block)
            def _():
                at = block * part
                fresh_kv[:, at : at + part] = mixed[count : count + fresh, :]
                fresh_kv[:, width + at : width + at + part] = mixed[count + fresh : count + 2 * fresh, :]


def mlp_kernel(h0, h1, h2, h3, p0, p1, p2, p3, w_up, w_down, o0, o1, o2, o3):
    count, part = h0.shape
    fresh = count // UNIT_GROUPS
    width = part * UNIT_GROUPS
    here = own_block()
    packs = (p0, p1, p2, p3)
    pieces = [h0[...]]
    for k, piece in enumerate((h1, h2, h3), start=1):
        value = piece[...].astype(F32)
        pieces.append(
            jnp.concatenate([value[(k ^ m) * fresh : (k ^ m) * fresh + fresh] for m in range(UNIT_GROUPS)], axis=0)
        )
    average = sum(jnp.sum(piece, axis=-1, keepdims=True) for piece in pieces) / width
    centred = [piece - average for piece in pieces]
    spread = sum(jnp.sum(piece * piece, axis=-1, keepdims=True) for piece in centred) / width
    scale = lax.rsqrt(spread + NORM_EPS)
    inner = jnp.zeros((count, w_up.shape[1]), F32)
    for k in range(UNIT_GROUPS):
        block = other_block(here, k)
        normed = centred[k] * scale
        middle = jnp.concatenate(
            [
                (
                    normed[m * fresh : (m + 1) * fresh] * (1.0 + mod_rows(packed, block, 4))
                    + mod_rows(packed, block, 3)
                ).astype(BF16)
                for m, packed in enumerate(packs)
            ],
            axis=0,
        )
        rows = pl.ds(pl.multiple_of(block * part, 32), part)
        inner += jnp.dot(middle, w_up[rows, :], preferred_element_type=F32)
    inner = jax.nn.gelu(inner, approximate=True).astype(BF16)
    partial_out = jnp.dot(inner, w_down[...], preferred_element_type=F32)
    for m, out in enumerate((o0, o1, o2, o3)):
        rows = slice(m * fresh, (m + 1) * fresh)
        gate = jnp.concatenate([mod_rows(packs[m], block, 5) for block in range(UNIT_GROUPS)], axis=1)
        own = pieces[0][rows]
        placed = jnp.concatenate(
            [jnp.where(here == block, own, 0.0) for block in range(UNIT_GROUPS)], axis=1
        )
        out[...] = (gate * partial_out[rows] + placed).astype(BF16)


def total_kernel(o0, o1, o2, o3, kept, leaving):
    half = kept.shape[0]
    section = lax.axis_index("section")
    for out, at in ((kept, section), (leaving, 1 - section)):
        rows = pl.ds(pl.multiple_of(at * half, half), half)
        out[...] = (
            (o0[rows, :].astype(F32) + o1[rows, :].astype(F32))
            + (o2[rows, :].astype(F32) + o3[rows, :].astype(F32))
        ).astype(BF16)


def final_kernel(time_index, time_gap, kept, arrived, mods, weight, noisy, next_rows, noise, denoised):
    first = lax.axis_index("section") == 0
    next_rows[...] = jnp.where(first, kept[...], arrived[...])
    rows = jnp.where(first, arrived[...], kept[...]).astype(F32)
    shifted = (layer_norm(rows) * (1.0 + mods[1:2, :]) + mods[0:1, :]).astype(BF16)
    repeated = jnp.dot(shifted, weight[...], preferred_element_type=F32)
    count, columns = repeated.shape
    channels = columns // count
    lane = lax.broadcasted_iota(jnp.int32, repeated.shape, 1)
    token = lax.broadcasted_iota(jnp.int32, repeated.shape, 0)
    mine = (lane >= token * channels) & (lane < (token + 1) * channels)
    value = jnp.sum(jnp.where(mine, repeated, 0.0), axis=0, keepdims=True)
    noise[...] = value
    now = jnp.full(value.shape, time_index[0], jnp.int32).astype(F32)
    before = jnp.full(value.shape, time_index[0] - time_gap[0], jnp.int32).astype(F32)
    now_bar, prev_bar = alpha_bar(now), alpha_bar(before)
    clean = (noisy[...] - jnp.sqrt(1.0 - now_bar) * value) / jnp.sqrt(now_bar)
    denoised[...] = jnp.sqrt(prev_bar) * clean + jnp.sqrt(1.0 - prev_bar) * value


def per_device(
    section_in,
    patch_index,
    stale_kv,
    modulation,
    final_mod,
    qkv_blocks,
    out_blocks,
    up_blocks,
    down_blocks,
    final_weight,
    noisy_latent,
    time_index,
    time_gap,
):
    shape = jax.ShapeDtypeStruct
    hidden, mods, stale = section_in[0, 0], modulation[0, 0], stale_kv[0, 0]
    fresh, width = hidden.shape
    part = width // UNIT_GROUPS
    half = fresh // 2
    count = UNIT_GROUPS * fresh
    others = range(1, UNIT_GROUPS)

    normed = call(norm_kernel, shape((fresh, width), BF16), hidden, mods)
    slots = [normed] + [swap(normed, k) for k in others]
    pack_rows = 2 * (stale.shape[0] - fresh) + fresh + UNIT_GROUPS * LANE_ROWS
    packs = call(
        pack_kernel,
        [shape((pack_rows, part), BF16)] * UNIT_GROUPS,
        patch_index,
        hidden,
        mods,
        stale,
        smem=1,
        scratch=[pltpu.VMEM((UNIT_GROUPS, pack_rows, part), BF16)],
    )
    packs = [packs[0]] + [swap(packs[k], k) for k in others]
    mixed = call(
        attend_kernel,
        [shape((count + 2 * fresh, part), BF16)] * UNIT_GROUPS,
        *slots,
        *packs,
        qkv_blocks[0, 0],
    )
    mixed = [mixed[0]] + [swap(mixed[k], k) for k in others]
    h1, sent, fresh_kv = call(
        project_kernel,
        [shape((count, part), F32), shape((count, part), BF16), shape((fresh, 2 * width), BF16)],
        *mixed,
        *packs,
        out_blocks[0, 0],
    )
    pieces = [h1] + [swap(sent, k) for k in others]
    parts = call(
        mlp_kernel,
        [shape((fresh, width), BF16)] * UNIT_GROUPS,
        *pieces,
        *packs,
        up_blocks[0, 0],
        down_blocks[0, 0],
    )
    parts = [parts[0]] + [swap(parts[k], k) for k in others]
    kept, leaving = call(total_kernel, [shape((half, width), BF16)] * 2, *parts)
    arrived = lax.ppermute(leaving, "section", [(0, 1), (1, 0)])
    next_rows, noise, denoised = call(
        final_kernel,
        [shape((half, width), BF16), shape(noisy_latent.shape, F32), shape(noisy_latent.shape, F32)],
        time_index,
        time_gap,
        kept,
        arrived,
        final_mod[0],
        jnp.tile(final_weight, (1, half)),
        noisy_latent,
        smem=2,
    )
    return (fresh_kv[None, None], next_rows[None], noise, denoised)


def solution(mesh):
    placed = (
        P("section", "req", None, None),
        P("section", "req"),
        P("section", "req", None, None),
        P("section", "req", None, None),
        P("req", None, None),
        P("section", "req", None, None),
        P("section", "req", None, None),
        P("section", "req", None, None),
        P("section", "req", None, None),
        P(),
        P("req", "section"),
        P("req"),
        P("req"),
    )
    return jax.shard_map(
        per_device,
        mesh=mesh,
        in_specs=placed,
        out_specs=(
            P("section", "req", None, None),
            P("req", "section", None),
            P("req", "section"),
            P("req", "section"),
        ),
        check_vma=False,
    )
```

```python
from functools import partial

import jax
import jax.numpy as jnp
from jax import lax
from jax.experimental import pallas as pl
from jax.experimental.pallas import tpu as pltpu
from jax.sharding import PartitionSpec as P

HEADS = 16
UNIT_GROUPS = 4


NORM_EPS = 1e-06
BETA_LOW = 0.0001
BETA_HIGH = 0.02

ORDER = tuple(reversed(range(UNIT_GROUPS)))

BF16 = jnp.bfloat16
F32 = jnp.float32
VMEM = pl.BlockSpec(memory_space=pltpu.VMEM)
HBM = pl.BlockSpec(memory_space=pltpu.HBM)
PARAMS = pltpu.CompilerParams(vmem_limit_bytes=12 * 1024 * 1024)


def layer_norm(values):
    average = jnp.mean(values, axis=-1, keepdims=True)
    centred = values - average
    spread = jnp.mean(centred * centred, axis=-1, keepdims=True)
    return centred * lax.rsqrt(spread + NORM_EPS)


def alpha_bar(moment):
    return jnp.exp(
        -(BETA_LOW * (moment + 1.0) + (BETA_HIGH - BETA_LOW) * moment * (moment + 1.0) / 1998.0)
    )


def own_block():
    return lax.rem(lax.axis_index("req"), UNIT_GROUPS)


def other_block(block, k):
    return lax.bitwise_xor(block, jnp.int32(k))


def swap(x, k):
    return lax.ppermute(x, "req", [(i, i ^ k) for i in range(lax.axis_size("req"))])


def swap_each(arrays):
    return [swap(array, k) if k else array for k, array in zip(ORDER, arrays)][::-1]


def call(body, outs, *args, far=(), scratch=(), micros=0.0, turn=True):
    specs = [HBM if i in far else VMEM for i in range(len(args))]
    args = [pltpu.with_memory_space_constraint(arg, pltpu.HBM) if i in far else arg for i, arg in enumerate(args)]
    way = -1 if turn else 1

    def turned(*refs):
        body(*refs[: len(args)][::way], *refs[len(args) :])

    return pl.pallas_call(
        turned,
        out_shape=outs,
        in_specs=specs[::way],
        out_specs=jax.tree.map(lambda _: VMEM, outs),
        scratch_shapes=list(scratch),
        compiler_params=PARAMS,
        cost_estimate=pl.CostEstimate(flops=int(micros * 1e9), bytes_accessed=0, transcendentals=0),
        name=body.__name__,
    )(*args[::way])


def cut(rows, count):
    part = rows.shape[1] // count
    return [rows[:, i * part : (i + 1) * part] for i in range(count)]


def beside(pieces):
    return jnp.concatenate(pieces, axis=1)


def below(pieces):
    return jnp.concatenate(pieces, axis=0)


def product(left, right_rows):
    return lax.dot_general(left, right_rows, (((1,), (1,)), ((), ())), preferred_element_type=F32)


MOD_ROWS = (0, 1, 2, 3, 4)
LOW_ROWS = (1, 2, 4)


def gather_kernel(hidden_far, mods_far, stale_far, packed, mods, stale, sems):
    fresh = hidden_far.shape[0]
    copies = [
        pltpu.make_async_copy(mods_far, mods, sems.at[0]),
        pltpu.make_async_copy(hidden_far, packed.at[pl.ds(0, fresh)], sems.at[1]),
        pltpu.make_async_copy(stale_far, stale, sems.at[2]),
    ]
    for copy in copies:
        copy.start()
    copies[0].wait()
    rows = [mods[i] for i in MOD_ROWS] + [mods[i] - mods[i].astype(BF16).astype(F32) for i in LOW_ROWS]
    packed[fresh:, :] = below(rows).astype(BF16)
    copies[1].wait()
    copies[2].wait()


def mod_row(packed, i):
    first = packed.shape[0] - len(MOD_ROWS) - len(LOW_ROWS)
    rows = packed[first:, :].astype(F32)
    row = rows[i : i + 1]
    if i in LOW_ROWS:
        at = len(MOD_ROWS) + LOW_ROWS.index(i)
        row = row + rows[at : at + 1]
    return row


def token_rows(packed):
    return packed[: packed.shape[0] - len(MOD_ROWS) - len(LOW_ROWS), :]


def factor_kernel(now, gap, factors):
    columns = factors.shape[1]
    now_bar = alpha_bar(jnp.broadcast_to(now[...], (1, columns)).astype(F32))
    prev_bar = alpha_bar(jnp.broadcast_to(now[...] - gap[...], (1, columns)).astype(F32))
    factors[0:1, :] = jnp.sqrt(1.0 - now_bar)
    factors[1:2, :] = jnp.sqrt(now_bar)
    factors[2:3, :] = jnp.sqrt(1.0 - prev_bar)
    factors[3:4, :] = jnp.sqrt(prev_bar)


def pack_kernel(stale, patch, *rest):
    *outs, packed = rest
    width = stale.shape[1] // 2
    part = width // UNIT_GROUPS
    fresh = 2 * outs[0].shape[0] // 3
    patches = stale.shape[0] // fresh
    at = patch[...]
    keys_values = [stale[i * fresh : (i + 1) * fresh, :] for i in range(patches)]
    kept = []
    for i in range(1, patches):
        rows = keys_values[i]
        for start in range(1, patches):
            rows = jnp.where(at == start, keys_values[(start + i) % patches], rows)
        kept.append(rows)
    keys = [cut(rows[:, :width], UNIT_GROUPS) for rows in kept]
    values = [cut(rows[:, width:], UNIT_GROUPS) for rows in kept]
    for block in range(UNIT_GROUPS):
        first = [rows[block] for rows in keys] + [values[0][block]]
        second = beside([rows[block] for rows in values[1:]])
        packed[block, :fresh, :] = beside(first)
        packed[block, fresh:, :] = beside([second[: fresh // 2], second[fresh // 2 :]])
    here = own_block()
    for k, out in zip(ORDER, outs):
        out[...] = packed[other_block(here, k)]


def unpack(packed):
    fresh = 2 * packed.shape[0] // 3
    first = cut(packed[:fresh, :], UNIT_GROUPS)
    second = cut(below(cut(packed[fresh:, :], 2)), 2)
    return first[:3], first[3:] + second


def join_kernel(t0, t1, t2, t3, weight, queries, keys, values, near, second, own):
    tokens = []
    for packed in (t0, t1, t2, t3):
        rows = layer_norm(token_rows(packed).astype(F32))
        tokens.append((rows * (1.0 + mod_row(packed, 1)) + mod_row(packed, 0)).astype(BF16))
    fresh = tokens[0].shape[0]
    joined = product(below(tokens), weight[...]).astype(BF16)
    q, k, v = cut(joined, 3)
    part = q.shape[1]
    heads = HEADS // UNIT_GROUPS
    inside = head_lanes(fresh, part)
    zero = jnp.zeros((fresh, part), BF16)
    for m in range(UNIT_GROUPS):
        rows = q[m * fresh : (m + 1) * fresh]
        for h in range(heads):
            at = (m * heads + h) * fresh
            queries[at : at + fresh, :] = jnp.where(inside[h], rows, zero)
    keys[...] = k
    values[...] = v
    pairs = [joined[m * fresh : (m + 1) * fresh, part:] for m in range(UNIT_GROUPS)]
    near[...] = beside([pairs[1], pairs[3]])
    second[...] = pairs[2]
    own[...] = pairs[0]


def head_lanes(rows, part):
    heads = HEADS // UNIT_GROUPS
    head_size = part // heads
    lane = lax.broadcasted_iota(jnp.int32, (rows, part), 1)
    return [(lane >= h * head_size) & (lane < (h + 1) * head_size) for h in range(heads)]


def attend_kernel(queries, k, v, p0, p1, p2, p3, sent):
    count, part = k.shape
    fresh = count // UNIT_GROUPS
    heads = HEADS // UNIT_GROUPS
    inside = head_lanes(fresh, part)
    scores = []
    values = []
    for m, packed in enumerate((p0, p1, p2, p3)):
        rows = slice(m * fresh, (m + 1) * fresh)
        stale_keys, stale_values = unpack(packed)
        spread = queries[m * heads * fresh : (m + 1) * heads * fresh, :]
        scores.append(product(spread, below(stale_keys + [k[rows, :]])))
        values.append(below(stale_values + [v[rows, :]]))
    scores = below(scores) * (part // heads) ** (-0.5)
    raised = jnp.exp(scores - jnp.max(scores, axis=-1, keepdims=True))
    probs = (raised * (1.0 / jnp.sum(raised, axis=-1, keepdims=True))).astype(BF16)
    mixed = []
    for m in range(UNIT_GROUPS):
        found = jnp.dot(probs[m * heads * fresh : (m + 1) * heads * fresh], values[m], preferred_element_type=F32)
        total = jnp.where(inside[0], found[:fresh], 0.0)
        for h in range(1, heads):
            total = jnp.where(inside[h], found[h * fresh : (h + 1) * fresh], total)
        mixed.append(total.astype(BF16))
    sent[...] = beside(mixed)


def place_blocks(columns, pieces):
    here = own_block()
    for k, piece in enumerate(pieces):
        slots = cut(piece[...], UNIT_GROUPS)
        columns[other_block(here, k)] = below([slots[k ^ m] for m in range(UNIT_GROUPS)])
    return beside([columns[block] for block in range(UNIT_GROUPS)])


def project_kernel(a0, a1, a2, a3, weight, near, sent, onward, columns):
    projected = product(place_blocks(columns, (a0, a1, a2, a3)), weight[...]).astype(BF16)
    fresh = sent.shape[0]
    onward[...] = near[...]
    sent[...] = beside([projected[m * fresh : (m + 1) * fresh] for m in range(UNIT_GROUPS)])


def relay_kernel(second, arrived, onward):
    onward[...] = beside([second[...], cut(arrived[...], 2)[1]])


def fresh_kernel(own, near, far, fresh_kv, columns):
    here = own_block()
    for k, rows in enumerate((own[...], cut(near[...], 2)[0], *cut(far[...], 2))):
        columns[other_block(here, k)] = rows
    pairs = [cut(columns[block], 2) for block in range(UNIT_GROUPS)]
    fresh_kv[...] = beside([pair[0] for pair in pairs] + [pair[1] for pair in pairs])


def mlp_kernel(h0, h1, h2, h3, t0, t1, t2, t3, w_up, w_down, *rest):
    *outs, home, columns = rest
    fresh = h0.shape[0]
    projected = place_blocks(columns, (h0, h1, h2, h3)).astype(F32)
    middle = []
    for m, packed in enumerate((t0, t1, t2, t3)):
        gated = mod_row(packed, 2) * projected[m * fresh : (m + 1) * fresh]
        values = token_rows(packed).astype(F32) + gated
        if m == 0:
            home[...] = values
        middle.append((layer_norm(values) * (1.0 + mod_row(packed, 4)) + mod_row(packed, 3)).astype(BF16))
    middle = below(middle)
    inner = jnp.dot(middle, w_up[...], preferred_element_type=F32)
    inner = jax.nn.gelu(inner, approximate=True).astype(BF16)
    partial_out = jnp.dot(inner, w_down[...], preferred_element_type=F32)
    for m, out in zip(ORDER, outs):
        out[...] = partial_out[m * fresh : (m + 1) * fresh].astype(BF16)


def total_kernel(o0, o1, o2, o3, home, mods, last_mods, weight, kept, noise, sent):
    half = kept.shape[0]
    section = lax.axis_index("section")
    columns = noise.shape[1]
    found = []
    for at in (section, 1 - section):
        rows = pl.ds(pl.multiple_of(at * half, half), half)
        total = (o0[rows, :].astype(F32) + o1[rows, :].astype(F32)) + (
            o2[rows, :].astype(F32) + o3[rows, :].astype(F32)
        )
        found.append((home[rows, :] + mods[5] * total).astype(BF16))
    kept[...] = found[0]
    sent[:half, :] = found[1]

    @pl.when(section == 1)
    def _():
        rows = below(found).astype(F32)
        shifted = (layer_norm(rows) * (1.0 + last_mods[1:2, :]) + last_mods[0:1, :]).astype(BF16)
        repeated = product(shifted, weight[...])
        channels = columns // half
        lane = lax.broadcasted_iota(jnp.int32, (half, columns), 1)
        token = lax.broadcasted_iota(jnp.int32, (half, columns), 0)
        mine = (lane >= token * channels) & (lane < (token + 1) * channels)
        own, other = [
            jnp.sum(jnp.where(mine, rows, 0.0), axis=0, keepdims=True) for rows in (repeated[:half], repeated[half:])
        ]
        noise[...] = own
        parts = []
        for _ in range(3):
            parts.append(other.astype(BF16).astype(F32))
            other = other - parts[-1]
        blank = jnp.zeros((sent.shape[0] - half - len(parts), columns), F32)
        sent[half:, :columns] = below(parts + [blank]).astype(BF16)


def final_kernel(factors, kept, arrived, own_noise, noisy, next_rows, noise, denoised):
    first = lax.axis_index("section") == 0
    half, columns = kept.shape[0], noise.shape[1]
    next_rows[...] = jnp.where(first, kept[...], arrived[:half, :])
    parts = arrived[half:, :columns].astype(F32)
    value = jnp.where(first, parts[0:1] + parts[1:2] + parts[2:3], own_noise[...])
    noise[...] = value
    clean = (noisy[...] - factors[0:1, :] * value) / factors[1:2, :]
    denoised[...] = factors[3:4, :] * clean + factors[2:3, :] * value


def per_device(
    section_in,
    patch_index,
    stale_kv,
    modulation,
    final_mod,
    qkv_blocks,
    out_blocks,
    up_blocks,
    down_blocks,
    final_weight,
    noisy_latent,
    time_index,
    time_gap,
):
    shape = jax.ShapeDtypeStruct
    hidden, stale = section_in[0, 0], stale_kv[0, 0]
    mods = modulation[0, 0][:, None, :]
    fresh, width = hidden.shape
    part = width // UNIT_GROUPS
    half = fresh // 2
    count = UNIT_GROUPS * fresh
    others = range(1, UNIT_GROUPS)

    packed, mods, stale = call(
        gather_kernel,
        [
            shape((fresh + len(MOD_ROWS) + len(LOW_ROWS), width), BF16),
            shape(mods.shape, F32),
            shape(stale.shape, BF16),
        ],
        hidden,
        mods,
        stale,
        far=range(3),
        scratch=[pltpu.SemaphoreType.DMA((3,))],
        micros=1.0,
    )
    slots = [packed] + [swap(packed, k) for k in others]
    pack_rows = fresh + fresh // 2
    packs = call(
        pack_kernel,
        [shape((pack_rows, width), BF16)] * UNIT_GROUPS,
        stale,
        patch_index,
        scratch=[pltpu.VMEM((UNIT_GROUPS, pack_rows, width), BF16)],
        micros=6.0,
    )
    factors = call(
        factor_kernel,
        shape((8, noisy_latent.shape[1]), F32),
        time_index[None],
        time_gap[None],
        micros=1.0,
    )
    packs = swap_each(packs)
    w_qkv = qkv_blocks[0, 0].T
    queries, keys, values, near, second, own = call(
        join_kernel,
        [
            shape((HEADS // UNIT_GROUPS * count, part), BF16),
            shape((count, part), BF16),
            shape((count, part), BF16),
            shape((fresh, width), BF16),
            shape((fresh, 2 * part), BF16),
            shape((fresh, 2 * part), BF16),
        ],
        *slots,
        w_qkv,
        micros=1.0,
    )
    sent = call(attend_kernel, shape((fresh, width), BF16), queries, keys, values, *packs, micros=2.0)
    mixed = [sent] + [swap(sent, k) for k in others]
    sent, near = call(
        project_kernel,
        [shape((fresh, width), BF16)] * 2,
        *mixed,
        out_blocks[0, 0].T,
        near,
        scratch=[pltpu.VMEM((UNIT_GROUPS, count, part), BF16)],
        micros=1.0,
    )
    pieces = [sent] + [swap(sent, k) for k in others]
    near = swap(near, 1)
    onward = call(relay_kernel, shape((fresh, width), BF16), second, near, micros=0.1)
    fresh_kv = call(
        fresh_kernel,
        shape((fresh, 2 * width), BF16),
        own,
        near,
        swap(onward, 2),
        scratch=[pltpu.VMEM((UNIT_GROUPS, fresh, 2 * part), BF16)],
        micros=1.0,
    )
    *parts, home = call(
        mlp_kernel,
        [shape((fresh, width), BF16)] * UNIT_GROUPS + [shape((fresh, width), F32)],
        *pieces,
        *slots,
        up_blocks[0, 0],
        down_blocks[0, 0],
        scratch=[pltpu.VMEM((UNIT_GROUPS, count, part), BF16)],
        micros=2.0,
    )
    parts = swap_each(parts)
    row = shape(noisy_latent.shape, F32)
    kept, own_noise, sent = call(
        total_kernel,
        [shape((half, width), BF16), row, shape((half + 16, width), BF16)],
        *parts,
        home,
        mods,
        final_mod[0],
        jnp.tile(final_weight.T, (half, 1)),
    )
    next_rows, noise, denoised = call(
        final_kernel,
        [shape((half, width), BF16), row, row],
        factors,
        kept,
        lax.ppermute(sent, "section", [(0, 1), (1, 0)]),
        own_noise,
        noisy_latent,
    )
    return (fresh_kv[None, None], next_rows[None], noise, denoised)


def solution(mesh):
    placed = (
        P("section", "req", None, None),
        P("section", "req"),
        P("section", "req", None, None),
        P("section", "req", None, None),
        P("req", None, None),
        P("section", "req", None, None),
        P("section", "req", None, None),
        P("section", "req", None, None),
        P("section", "req", None, None),
        P(),
        P("req", "section"),
        P("req"),
        P("req"),
    )
    return jax.shard_map(
        per_device,
        mesh=mesh,
        in_specs=placed,
        out_specs=(
            P("section", "req", None, None),
            P("req", "section", None),
            P("req", "section"),
            P("req", "section"),
        ),
        check_vma=False,
    )
```

```python
from functools import partial

import jax
import jax.numpy as jnp
from jax import lax
from jax.experimental import pallas as pl
from jax.experimental.pallas import tpu as pltpu
from jax.sharding import PartitionSpec as P

HEADS = 16
UNIT_GROUPS = 4


NORM_EPS = 1e-06
BETA_LOW = 0.0001
BETA_HIGH = 0.02

ORDER = tuple(reversed(range(UNIT_GROUPS)))

BF16 = jnp.bfloat16
F32 = jnp.float32
VMEM = pl.BlockSpec(memory_space=pltpu.VMEM)
HBM = pl.BlockSpec(memory_space=pltpu.HBM)
PARAMS = pltpu.CompilerParams(vmem_limit_bytes=12 * 1024 * 1024)


def layer_norm(values):
    average = jnp.mean(values, axis=-1, keepdims=True)
    centred = values - average
    spread = jnp.mean(centred * centred, axis=-1, keepdims=True)
    return centred * lax.rsqrt(spread + NORM_EPS)


def alpha_bar(moment):
    return jnp.exp(
        -(BETA_LOW * (moment + 1.0) + (BETA_HIGH - BETA_LOW) * moment * (moment + 1.0) / 1998.0)
    )


def own_block():
    return lax.rem(lax.axis_index("req"), UNIT_GROUPS)


def other_block(block, k):
    return lax.bitwise_xor(block, jnp.int32(k))


def swap(x, k):
    return lax.ppermute(x, "req", [(i, i ^ k) for i in range(lax.axis_size("req"))])


def swap_each(arrays):
    return [swap(array, k) if k else array for k, array in zip(ORDER, arrays)][::-1]


def call(body, outs, *args, far=(), scratch=(), micros=0.0, turn=True):
    specs = [HBM if i in far else VMEM for i in range(len(args))]
    args = [pltpu.with_memory_space_constraint(arg, pltpu.HBM) if i in far else arg for i, arg in enumerate(args)]
    way = -1 if turn else 1

    def turned(*refs):
        body(*refs[: len(args)][::way], *refs[len(args) :])

    return pl.pallas_call(
        turned,
        out_shape=outs,
        in_specs=specs[::way],
        out_specs=jax.tree.map(lambda _: VMEM, outs),
        scratch_shapes=list(scratch),
        compiler_params=PARAMS,
        cost_estimate=pl.CostEstimate(flops=int(micros * 1e9), bytes_accessed=0, transcendentals=0),
        name=body.__name__,
    )(*args[::way])


def cut(rows, count):
    part = rows.shape[1] // count
    return [rows[:, i * part : (i + 1) * part] for i in range(count)]


def beside(pieces):
    return jnp.concatenate(pieces, axis=1)


def below(pieces):
    return jnp.concatenate(pieces, axis=0)


def product(left, right_rows):
    return lax.dot_general(left, right_rows, (((1,), (1,)), ((), ())), preferred_element_type=F32)


MOD_ROWS = (0, 1, 2, 3, 4)
LOW_ROWS = (1, 2, 4)


def gather_kernel(hidden_far, mods_far, stale_far, packed, mods, stale, sems):
    fresh = hidden_far.shape[0]
    copies = [
        pltpu.make_async_copy(mods_far, mods, sems.at[0]),
        pltpu.make_async_copy(hidden_far, packed.at[pl.ds(0, fresh)], sems.at[1]),
        pltpu.make_async_copy(stale_far, stale, sems.at[2]),
    ]
    for copy in copies:
        copy.start()
    copies[0].wait()
    rows = [mods[i] for i in MOD_ROWS] + [mods[i] - mods[i].astype(BF16).astype(F32) for i in LOW_ROWS]
    packed[fresh:, :] = below(rows).astype(BF16)
    copies[1].wait()
    copies[2].wait()


def mod_row(packed, i):
    first = packed.shape[0] - len(MOD_ROWS) - len(LOW_ROWS)
    rows = packed[first:, :].astype(F32)
    row = rows[i : i + 1]
    if i in LOW_ROWS:
        at = len(MOD_ROWS) + LOW_ROWS.index(i)
        row = row + rows[at : at + 1]
    return row


def token_rows(packed):
    return packed[: packed.shape[0] - len(MOD_ROWS) - len(LOW_ROWS), :]


def factor_kernel(now, gap, factors):
    columns = factors.shape[1]
    now_bar = alpha_bar(jnp.broadcast_to(now[...], (1, columns)).astype(F32))
    prev_bar = alpha_bar(jnp.broadcast_to(now[...] - gap[...], (1, columns)).astype(F32))
    factors[0:1, :] = jnp.sqrt(1.0 - now_bar)
    factors[1:2, :] = jnp.sqrt(now_bar)
    factors[2:3, :] = jnp.sqrt(1.0 - prev_bar)
    factors[3:4, :] = jnp.sqrt(prev_bar)


def pack_kernel(stale, patch, *rest):
    outs = rest
    width = stale.shape[1] // 2
    part = width // UNIT_GROUPS
    fresh = 2 * outs[0].shape[0] // 3
    patches = stale.shape[0] // fresh
    at = patch[...]
    keys_values = [stale[i * fresh : (i + 1) * fresh, :] for i in range(patches)]
    kept = []
    for i in range(1, patches):
        rows = keys_values[i]
        for start in range(1, patches):
            rows = jnp.where(at == start, keys_values[(start + i) % patches], rows)
        kept.append(rows)
    keys = [cut(rows[:, :width], UNIT_GROUPS) for rows in kept]
    values = [cut(rows[:, width:], UNIT_GROUPS) for rows in kept]
    whole = []
    for block in range(UNIT_GROUPS):
        second = beside([rows[block] for rows in values[1:]])
        first = beside([rows[block] for rows in keys] + [values[0][block]])
        whole.append((first, beside([second[: fresh // 2], second[fresh // 2 :]])))
    here = own_block()
    for block in range(UNIT_GROUPS):

        @pl.when(here == block)
        def _():
            for k, out in zip(ORDER, outs):
                out[:fresh, :], out[fresh:, :] = whole[block ^ k]


def unpack(packed):
    fresh = 2 * packed.shape[0] // 3
    first = cut(packed[:fresh, :], UNIT_GROUPS)
    second = cut(below(cut(packed[fresh:, :], 2)), 2)
    return first[:3], first[3:] + second


def join_kernel(t0, t1, t2, t3, p0, weight, queries, keys, values, near, second, own, mixed):
    tokens = []
    for packed in (t0, t1, t2, t3):
        rows = layer_norm(token_rows(packed).astype(F32))
        tokens.append((rows * (1.0 + mod_row(packed, 1)) + mod_row(packed, 0)).astype(BF16))
    fresh = tokens[0].shape[0]
    joined = product(below(tokens), weight[...]).astype(BF16)
    q, k, v = cut(joined, 3)
    part = q.shape[1]
    heads = HEADS // UNIT_GROUPS
    inside = head_lanes(fresh, part)
    zero = jnp.zeros((fresh, part), BF16)
    for m in range(UNIT_GROUPS):
        rows = q[m * fresh : (m + 1) * fresh]
        for h in range(heads):
            at = (m * heads + h) * fresh
            queries[at : at + fresh, :] = jnp.where(inside[h], rows, zero)
    keys[...] = k
    values[...] = v
    pairs = [joined[m * fresh : (m + 1) * fresh, part:] for m in range(UNIT_GROUPS)]
    near[...] = beside([pairs[1], pairs[3]])
    second[...] = pairs[2]
    own[...] = pairs[0]
    spread = below([jnp.where(inside[h], q[:fresh], zero) for h in range(heads)])
    mixed[...] = attention(spread, (p0,), [k[:fresh]], [v[:fresh]])[0]


def head_lanes(rows, part):
    heads = HEADS // UNIT_GROUPS
    head_size = part // heads
    lane = lax.broadcasted_iota(jnp.int32, (rows, part), 1)
    return [(lane >= h * head_size) & (lane < (h + 1) * head_size) for h in range(heads)]


def attention(queries, packs, fresh_keys, fresh_values):
    fresh, part = fresh_keys[0].shape
    heads = HEADS // UNIT_GROUPS
    span = heads * fresh
    inside = head_lanes(fresh, part)
    stale = [unpack(packed) for packed in packs]
    scores = []
    for m, ((stale_keys, _), k) in enumerate(zip(stale, fresh_keys)):
        scores.append(product(queries[m * span : (m + 1) * span], below(stale_keys + [k])))
    scores = below(scores) * (part // heads) ** (-0.5)
    raised = jnp.exp(scores - jnp.max(scores, axis=-1, keepdims=True)).astype(BF16)
    ones = jnp.ones((scores.shape[1], part // 3), BF16)
    mixed = []
    for m, ((_, stale_values), v) in enumerate(zip(stale, fresh_values)):
        rows = beside([below(stale_values + [v]), ones])
        found = jnp.dot(raised[m * span : (m + 1) * span], rows, preferred_element_type=F32)
        found = found[:, :part] * (1.0 / found[:, part : part + 1])
        total = jnp.where(inside[0], found[:fresh], 0.0)
        for h in range(1, heads):
            total = jnp.where(inside[h], found[h * fresh : (h + 1) * fresh], total)
        mixed.append(total.astype(BF16))
    return mixed


def attend_kernel(queries, k, v, own, p1, p2, p3, sent):
    fresh = own.shape[0]
    rows = [slice(m * fresh, (m + 1) * fresh) for m in range(1, UNIT_GROUPS)]
    span = queries.shape[0] // UNIT_GROUPS
    mixed = attention(queries[span:, :], (p1, p2, p3), [k[row, :] for row in rows], [v[row, :] for row in rows])
    sent[...] = beside([own[...]] + mixed)


def place_blocks(columns, pieces):
    here = own_block()
    fresh, width = pieces[0].shape
    part = width // UNIT_GROUPS
    for block in range(UNIT_GROUPS):

        @pl.when(here == block)
        def _():
            slots = [cut(piece[...], UNIT_GROUPS) for piece in pieces]
            for m in range(UNIT_GROUPS):
                columns[m * fresh : (m + 1) * fresh, :] = beside(
                    [slots[k][k ^ m] for k in [block ^ other for other in range(UNIT_GROUPS)]]
                )

    return columns[...]


def project_kernel(a0, a1, a2, a3, weight, sent, columns):
    projected = product(place_blocks(columns, (a0, a1, a2, a3)), weight[...]).astype(BF16)
    fresh = sent.shape[0]
    sent[...] = beside([projected[m * fresh : (m + 1) * fresh] for m in range(UNIT_GROUPS)])


def hold_kernel(rows, arrived, out):
    del arrived
    out[...] = rows[...]


def relay_kernel(second, arrived, onward):
    onward[...] = beside([second[...], cut(arrived[...], 2)[1]])


def fresh_kernel(own, near, far, fresh_kv, columns):
    here = own_block()
    for k, rows in enumerate((own[...], cut(near[...], 2)[0], *cut(far[...], 2))):
        columns[other_block(here, k)] = rows
    pairs = [cut(columns[block], 2) for block in range(UNIT_GROUPS)]
    fresh_kv[...] = beside([pair[0] for pair in pairs] + [pair[1] for pair in pairs])


def mlp_kernel(h0, h1, h2, h3, t0, t1, t2, t3, w_up, w_down, *rest):
    *outs, home, columns = rest
    fresh = h0.shape[0]
    projected = place_blocks(columns, (h0, h1, h2, h3)).astype(F32)
    middle = []
    for m, packed in enumerate((t0, t1, t2, t3)):
        gated = mod_row(packed, 2) * projected[m * fresh : (m + 1) * fresh]
        values = token_rows(packed).astype(F32) + gated
        if m == 0:
            home[...] = values
        middle.append((layer_norm(values) * (1.0 + mod_row(packed, 4)) + mod_row(packed, 3)).astype(BF16))
    middle = below(middle)
    inner = jnp.dot(middle, w_up[...], preferred_element_type=F32)
    inner = jax.nn.gelu(inner, approximate=True).astype(BF16)
    partial_out = jnp.dot(inner, w_down[...], preferred_element_type=F32)
    for m, out in zip(ORDER, outs):
        out[...] = partial_out[m * fresh : (m + 1) * fresh].astype(BF16)


def total_kernel(o0, o1, o2, o3, home, mods, last_mods, weight, fresh_kv, kept, noise, sent):
    del fresh_kv
    half = kept.shape[0]
    section = lax.axis_index("section")
    columns = noise.shape[1]
    found = []
    for at in (section, 1 - section):
        rows = pl.ds(pl.multiple_of(at * half, half), half)
        total = (o0[rows, :].astype(F32) + o1[rows, :].astype(F32)) + (
            o2[rows, :].astype(F32) + o3[rows, :].astype(F32)
        )
        found.append((home[rows, :] + mods[5] * total).astype(BF16))
    kept[...] = found[0]
    sent[:half, :] = found[1]

    @pl.when(section == 1)
    def _():
        rows = below(found).astype(F32)
        shifted = (layer_norm(rows) * (1.0 + last_mods[1:2, :]) + last_mods[0:1, :]).astype(BF16)
        repeated = product(shifted, weight[...])
        channels = columns // half
        lane = lax.broadcasted_iota(jnp.int32, (half, columns), 1)
        token = lax.broadcasted_iota(jnp.int32, (half, columns), 0)
        mine = (lane >= token * channels) & (lane < (token + 1) * channels)
        own, other = [
            jnp.sum(jnp.where(mine, rows, 0.0), axis=0, keepdims=True) for rows in (repeated[:half], repeated[half:])
        ]
        noise[...] = own
        parts = []
        for _ in range(3):
            parts.append(other.astype(BF16).astype(F32))
            other = other - parts[-1]
        blank = jnp.zeros((sent.shape[0] - half - len(parts), columns), F32)
        sent[half:, :columns] = below(parts + [blank]).astype(BF16)


def final_kernel(factors, kept, arrived, own_noise, noisy, next_rows, noise, denoised):
    first = lax.axis_index("section") == 0
    half, columns = kept.shape[0], noise.shape[1]
    next_rows[...] = jnp.where(first, kept[...], arrived[:half, :])
    parts = arrived[half:, :columns].astype(F32)
    value = jnp.where(first, parts[0:1] + parts[1:2] + parts[2:3], own_noise[...])
    noise[...] = value
    clean = (noisy[...] - factors[0:1, :] * value) / factors[1:2, :]
    denoised[...] = factors[3:4, :] * clean + factors[2:3, :] * value


def per_device(
    section_in,
    patch_index,
    stale_kv,
    modulation,
    final_mod,
    qkv_blocks,
    out_blocks,
    up_blocks,
    down_blocks,
    final_weight,
    noisy_latent,
    time_index,
    time_gap,
):
    shape = jax.ShapeDtypeStruct
    hidden, stale = section_in[0, 0], stale_kv[0, 0]
    mods = modulation[0, 0][:, None, :]
    fresh, width = hidden.shape
    part = width // UNIT_GROUPS
    half = fresh // 2
    count = UNIT_GROUPS * fresh
    others = range(1, UNIT_GROUPS)

    packed, mods, stale = call(
        gather_kernel,
        [
            shape((fresh + len(MOD_ROWS) + len(LOW_ROWS), width), BF16),
            shape(mods.shape, F32),
            shape(stale.shape, BF16),
        ],
        hidden,
        mods,
        stale,
        far=range(3),
        scratch=[pltpu.SemaphoreType.DMA((3,))],
        micros=1.0,
    )
    slots = [packed] + [swap(packed, k) for k in others]
    pack_rows = fresh + fresh // 2
    packs = call(
        pack_kernel,
        [shape((pack_rows, width), BF16)] * UNIT_GROUPS,
        stale,
        patch_index,
        micros=6.0,
    )
    factors = call(
        factor_kernel,
        shape((8, noisy_latent.shape[1]), F32),
        time_index[None],
        time_gap[None],
        micros=1.0,
    )
    packs = swap_each(packs)
    w_qkv = qkv_blocks[0, 0].T
    queries, keys, values, near, second, own, mixed = call(
        join_kernel,
        [
            shape((HEADS // UNIT_GROUPS * count, part), BF16),
            shape((count, part), BF16),
            shape((count, part), BF16),
            shape((fresh, width), BF16),
            shape((fresh, 2 * part), BF16),
            shape((fresh, 2 * part), BF16),
            shape((fresh, part), BF16),
        ],
        *slots,
        packs[0],
        w_qkv,
        micros=1.0,
    )
    sent = call(attend_kernel, shape((fresh, width), BF16), queries, keys, values, mixed, *packs[1:], micros=2.0)
    mixed = [sent] + [swap(sent, k) for k in others]
    sent = call(
        project_kernel,
        shape((fresh, width), BF16),
        *mixed,
        out_blocks[0, 0].T,
        scratch=[pltpu.VMEM((count, width), BF16)],
        micros=1.0,
    )
    pieces = [sent] + [swap(sent, k) for k in others]
    near = call(hold_kernel, shape((fresh, width), BF16), near, mixed[3], micros=0.1)
    near = swap(near, 1)
    onward = call(relay_kernel, shape((fresh, width), BF16), second, near, micros=0.1)
    fresh_kv = call(
        fresh_kernel,
        shape((fresh, 2 * width), BF16),
        own,
        near,
        swap(onward, 2),
        scratch=[pltpu.VMEM((UNIT_GROUPS, fresh, 2 * part), BF16)],
        micros=1.0,
    )
    *parts, home = call(
        mlp_kernel,
        [shape((fresh, width), BF16)] * UNIT_GROUPS + [shape((fresh, width), F32)],
        *pieces,
        *slots,
        up_blocks[0, 0],
        down_blocks[0, 0],
        scratch=[pltpu.VMEM((count, width), BF16)],
        micros=2.0,
    )
    parts = swap_each(parts)
    row = shape(noisy_latent.shape, F32)
    kept, own_noise, sent = call(
        total_kernel,
        [shape((half, width), BF16), row, shape((half + 16, width), BF16)],
        *parts,
        home,
        mods,
        final_mod[0],
        jnp.tile(final_weight.T, (half, 1)),
        fresh_kv,
        far=(8,),
    )
    next_rows, noise, denoised = call(
        final_kernel,
        [shape((half, width), BF16), row, row],
        factors,
        kept,
        lax.ppermute(sent, "section", [(0, 1), (1, 0)]),
        own_noise,
        noisy_latent,
    )
    return (fresh_kv[None, None], next_rows[None], noise, denoised)


def solution(mesh):
    placed = (
        P("section", "req", None, None),
        P("section", "req"),
        P("section", "req", None, None),
        P("section", "req", None, None),
        P("req", None, None),
        P("section", "req", None, None),
        P("section", "req", None, None),
        P("section", "req", None, None),
        P("section", "req", None, None),
        P(),
        P("req", "section"),
        P("req"),
        P("req"),
    )
    return jax.shard_map(
        per_device,
        mesh=mesh,
        in_specs=placed,
        out_specs=(
            P("section", "req", None, None),
            P("req", "section", None),
            P("req", "section"),
            P("req", "section"),
        ),
        check_vma=False,
    )
```
